32 devices in a mesh: shard: 4 (over y, x), dp: 4 (over z), tensor: 2 (over core).
Axes of the slice: x: 2, y: 2, z: 4, core: 2. Of those that a mesh axis runs over, the one named last changes fastest.
Arguments:
- tokens: bfloat16 [9456, 768], P(('shard', 'dp')), may hold values from -6 to 6
- routes: int32 [2, 9456, 2], P(None, ('shard', 'dp')), may hold values from 0 to 7, all different within a row; in each aligned block of 591 rows (0 to 590, 591 to 1181, ..., all dimensions but the last counted through in order) at most 185 rows name the same one
- w_qkv: bfloat16 [2, 768, 3, 768], P(None, ('shard', 'dp'), None, 'tensor'), may hold values from -0.21875 to 0.21875
- w_out: bfloat16 [2, 768, 768], P(None, ('shard', 'dp'), 'tensor'), may hold values from -1.25 to 1.25
- w_router: bfloat16 [2, 768, 8], P(None, ('shard', 'dp')), may hold values from -0.15625 to 0.15625
- ln_gain: bfloat16 [2, 768, 2], P(None, ('shard', 'dp')), may hold values from 0.5 to 1.5
- ln_shift: bfloat16 [2, 768, 2], P(None, ('shard', 'dp')), may hold values from -0.8984375 to 0.8984375
- expert_in: bfloat16 [2, 8, 768, 3072], P(None, 'shard', 'dp', 'tensor'), may hold values from -0.21875 to 0.21875
- expert_out: bfloat16 [2, 8, 768, 3072], P(None, 'shard', 'dp', 'tensor'), may hold values from -0.109375 to 0.109375
- cotangent: bfloat16 [9456, 768], P(('shard', 'dp')), may hold values from -6 to 6
Outputs:
- mixed: bfloat16 [9456, 768], P(('shard', 'dp'))
- tokens_grad: float32 [9456, 768], P(('shard', 'dp'))
- w_qkv_grad: float32 [2, 768, 3, 768], P(None, ('shard', 'dp'), None, 'tensor')
- w_out_grad: float32 [2, 768, 768], P(None, ('shard', 'dp'), 'tensor')
- w_router_grad: float32 [2, 768, 8], P(None, ('shard', 'dp'))
- ln_gain_grad: float32 [2, 768, 2], P(None, ('shard', 'dp'))
- ln_shift_grad: float32 [2, 768], P(None, ('shard', 'dp'))
- second_shift_grad: float32 [2, 768], P(None, ('shard', 'dp'))
- expert_in_grad: float32 [2, 8, 768, 3072], P(None, 'shard', 'dp', 'tensor')
- expert_out_grad: float32 [2, 8, 768, 3072], P(None, 'shard', 'dp', 'tensor')
The draws below stay inside these ranges and needn't reach their ends.
Inputs may be any that keep to these rules, and one draw needn't show every extreme that they name: `routes`: in the rows of one index of shard and dp and one block, no expert is named more than 185 times; a token's two experts differ.
All inputs are finite; a program needn't handle non-finite values.
Results may differ from the reference program's by a relative error of at most 0.02.
Values may be sent and summed in bfloat16 or wider, within the bound.
A program may use at most 256 MiB of HBM per device.

```python
import math
from functools import partial
import jax
import jax.numpy as jnp
import numpy as np
from jax import lax

D = 768
HEADS = 12
HEAD_DIM = 64
FF = 3072
SEQ = 197
LAYERS = 2
IMG_DEV = 3
EXPERTS = 8
TOK_DEV = 591
TOKENS = 9456
CAP = 185
N_SHARD = 4
N_DP = 4


def block_levels(rng, dims, split, low, largest):
    level = 1.0
    for axis_at, parts in split:
        steps = jax.random.uniform(jax.random.fold_in(jax.random.fold_in(rng, 6), axis_at), (parts,), jnp.float32, low / len(split), largest / len(split))
        level = level * jnp.repeat(jnp.exp(steps), dims[axis_at] // parts).reshape((-1,) + (1,) * (len(dims) - 1 - axis_at))
    return level


def shared_out(own_key, own, number, rows, amount, top, reach, slope):
    sequence = jax.random.permutation(own_key, amount)
    crowded, ordinary = portions_of(amount, rows * top, reach, slope, True), portions_of(amount, rows * top, reach, slope, False)
    places = jnp.arange(amount)

    def named(sizes, turn):
        used = int((sizes > 0).sum())
        fixed = max(1, used // 4)
        moved = fixed + (places - fixed + turn * (used - fixed)) % max(1, amount - fixed)
        return jnp.zeros((amount,), jnp.int32).at[sequence[jnp.where(places < fixed, places, moved)]].set(jnp.asarray(sizes, jnp.int32))

    sizes = jnp.where(number % 4 == 0, named(crowded, number // 4), named(ordinary, number - number // 4 - 1))
    mixed = jax.random.permutation(jax.random.fold_in(own, 3), amount)
    donor, taker = mixed[0:amount // 2 * 2:2], mixed[1:amount // 2 * 2:2]
    room = jnp.minimum(sizes[donor] - 1, reach - sizes[taker]) // 2
    room = jnp.where((donor == sequence[0]) | (taker == sequence[0]) | (sizes[taker] == 0), 0, jnp.maximum(room, 0))
    moved = jax.random.randint(jax.random.fold_in(own, 4), (amount // 2,), 0, 1 << 20) % (room + 1)
    sizes = sizes.at[donor].add(-moved).at[taker].add(moved)
    members = jnp.searchsorted(jnp.cumsum(sizes), jnp.arange(rows * top), side="right").astype(jnp.int32)
    listing = members.reshape(top, rows).T
    listing = listing[jax.random.permutation(jax.random.fold_in(own, 1), rows)]
    turn = jax.random.randint(jax.random.fold_in(own, 2), (rows, 1), 0, top)
    return jnp.take_along_axis(listing, (jnp.arange(top)[None, :] + turn) % top, axis=1)


def portions_of(number_of, total, most, skew, full):
    loads = [(1 << 20) // math.isqrt(rank ** skew) + 1 for rank in range(1, number_of + 1)]
    largest = most if full else min(most, max(-(-total // number_of), total * loads[0] // sum(loads)))
    least = 1 if total - largest >= number_of - 1 else 0
    counts, surplus = [largest] + [least] * (number_of - 1), total - largest - least * (number_of - 1)
    while surplus > 0:
        candidates = [i for i in range(1, number_of) if counts[i] < largest] or [i for i in range(1, number_of) if counts[i] < most]
        pool, budget = sum([loads[i] for i in candidates]), surplus
        for i in candidates:
            extra = min(most - counts[i], max(1, budget * loads[i] // pool), surplus)
            counts[i] = counts[i] + extra
            surplus = surplus - extra
    return np.array(counts)


def normal_values(key, shape, deviation, reach, cuts=(), kind=jnp.bfloat16):
    drawn = jax.random.normal(key, shape, jnp.float32) * deviation
    if len(cuts) > 0:
        drawn = block_levels(key, shape, cuts, -0.22, 0.18) * drawn
    return jnp.clip(drawn, min=-reach, max=reach).astype(kind)


def setup_inputs(seed: int = 0) -> dict:
    key_of = jax.random.split(jax.random.key(seed), 11)
    tokens = normal_values(key_of[0], (TOKENS, D), 1.0, 6.0, ((0, 16),))
    routes_keys = jax.random.split(jax.random.fold_in(key_of[1], 1), LAYERS * TOKENS // TOK_DEV)
    routes_turns = jax.random.permutation(jax.random.fold_in(key_of[1], 3), LAYERS * TOKENS // TOK_DEV)
    routes = jax.vmap(lambda own, number: shared_out(jax.random.fold_in(key_of[1], 2), own, number, TOK_DEV, EXPERTS, 2, CAP, 1))(routes_keys, routes_turns).reshape((LAYERS, TOKENS, 2))
    w_qkv = normal_values(key_of[2], (LAYERS, D, 3, D), D ** -0.5, 0.21875, ((1, 16), (3, 2)))
    w_out = normal_values(key_of[3], (LAYERS, D, D), (D // 32) ** -0.5, 1.25, ((1, 16), (2, 2)))
    w_router = normal_values(key_of[4], (LAYERS, D, EXPERTS), (2 * D) ** -0.5, 0.15625, ((1, 16),))
    ln_gain = jnp.clip(1.0 + 0.1 * jax.random.normal(key_of[5], (LAYERS, D, 2), jnp.float32), 0.5, 1.5).astype(jnp.bfloat16)
    ln_shift = normal_values(key_of[6], (LAYERS, D, 2), 0.15, 0.8984375, ((1, 16),))
    expert_in = normal_values(key_of[7], (LAYERS, EXPERTS, D, FF), D ** -0.5, 0.21875, ((1, 4), (2, 4), (3, 2)))
    expert_out = normal_values(key_of[8], (LAYERS, EXPERTS, D, FF), FF ** -0.5, 0.109375, ((1, 4), (2, 4), (3, 2)))
    cotangent = normal_values(key_of[9], (TOKENS, D), 1.0, 6.0, ((0, 16),))
    return {"tokens": tokens, "routes": routes, "w_qkv": w_qkv, "w_out": w_out, "w_router": w_router, "ln_gain": ln_gain, "ln_shift": ln_shift, "expert_in": expert_in, "expert_out": expert_out, "cotangent": cotangent}


@jax.custom_vjp
def low(v):
    return lax.optimization_barrier(v.astype(jnp.bfloat16)).astype(jnp.float32)

@jax.custom_vjp
def low_back(v):
    return v

def low_keep(v):
    return (low(v), None)

def low_pass(kept, grad):
    return (grad,)

def back_keep(v):
    return (v, None)

def back_low(kept, grad):
    return (low(grad),)
low.defvjp(low_keep, low_pass)
low_back.defvjp(back_keep, back_low)

def exact_dot(left, right):
    return jnp.dot(left, right, precision=lax.Precision.HIGHEST)

def exact_sum(form, left, right):
    return jnp.einsum(form, left, right, precision=lax.Precision.HIGHEST)

def norm_rows(values, gain_vec, shift_vec):
    row_mean = lax.optimization_barrier(jnp.mean(values, axis=-1, keepdims=True))
    centred = values - row_mean
    variance = lax.optimization_barrier(jnp.mean(centred * centred, axis=-1, keepdims=True))
    return centred * lax.rsqrt(variance + 1e-06) * gain_vec + shift_vec

def softmax_last(scores):
    row_max = lax.optimization_barrier(jnp.max(scores, axis=-1, keepdims=True))
    exponent = jnp.exp(scores - row_max)
    return exponent / lax.optimization_barrier(jnp.sum(exponent, axis=-1, keepdims=True))

def attend_group(normed, proj_qkv, proj_out):
    packed = low(low_back(exact_sum('td,dcf->tcf', normed, proj_qkv)))
    packed = packed.reshape(IMG_DEV, SEQ, 3, HEADS, HEAD_DIM)
    scores = low_back(exact_sum('bqhd,bkhd->bhqk', packed[:, :, 0], packed[:, :, 1]) * HEAD_DIM ** (-0.5))
    weights = low(softmax_last(scores))
    heads_out = exact_sum('bhqk,bkhd->bqhd', weights, packed[:, :, 2])
    heads_out = low(low_back(heads_out.reshape(TOK_DEV, D)))
    return low_back(exact_sum('tf,of->to', heads_out, proj_out))

def route_slots(route_rows):
    flat_ids = route_rows.reshape(-1)
    onehot_hits = (flat_ids[:, None] == jnp.arange(EXPERTS, dtype=jnp.int32)[None, :]).astype(jnp.int32)
    earlier = jnp.cumsum(onehot_hits, axis=0, dtype=jnp.int32) - onehot_hits
    return flat_ids * CAP + lax.optimization_barrier(jnp.sum(earlier * onehot_hits, axis=1))

def place_rows(dest_rows, copies):
    return jnp.zeros((EXPERTS * CAP, D), jnp.float32).at[dest_rows].set(copies)

def take_rows(table, dest_rows):
    return table[dest_rows]

def expert_apply(inputs):
    rows_in, weight_in, weight_down = inputs
    pre_act = low_back(exact_dot(rows_in, weight_in))
    act_low = low(jax.nn.gelu(pre_act, approximate=False))
    return low_back(exact_sum('rf,df->rd', act_low, weight_down))

def mixture(normed, route_ids, router, weight_in, weight_down):
    groups = N_SHARD * N_DP
    act_in = low(normed)
    logits = exact_dot(act_in, router)
    onehot_hits = (route_ids[:, :, None] == jnp.arange(EXPERTS, dtype=jnp.int32)[None, None, :]).astype(jnp.float32)
    chosen = lax.optimization_barrier(jnp.sum(onehot_hits * logits[:, None, :], axis=-1))
    gate_probs = softmax_last(chosen)
    dest_rows = jax.vmap(route_slots)(route_ids.reshape(groups, TOK_DEV, 2))
    copies = jnp.repeat(act_in.reshape(groups, TOK_DEV, D), 2, axis=1)
    buffers = jax.vmap(place_rows)(dest_rows, copies)
    expert_rows = buffers.reshape(groups, EXPERTS, CAP, D).transpose(1, 0, 2, 3).reshape(EXPERTS, groups * CAP, D)
    outputs = lax.map(jax.checkpoint(expert_apply), (expert_rows, weight_in, weight_down))
    outputs = outputs.reshape(EXPERTS, groups, CAP, D).transpose(1, 0, 2, 3).reshape(groups, EXPERTS * CAP, D)
    token_out = jax.vmap(take_rows)(outputs, dest_rows).reshape(TOKENS, 2, D)
    return lax.optimization_barrier(jnp.sum(gate_probs[:, :, None] * token_out, axis=1))

def block(stream, route_ids, proj_qkv, proj_out, router, gain_pair, shift_pair, weight_in, weight_down):
    groups = N_SHARD * N_DP
    normed = low(norm_rows(stream, gain_pair[:, 0], shift_pair[:, 0]))
    attend = jax.checkpoint(partial(attend_group, proj_qkv=proj_qkv, proj_out=proj_out))
    attention = lax.map(attend, normed.reshape(groups, TOK_DEV, D)).reshape(TOKENS, D)
    middle = stream + attention
    second = norm_rows(middle, gain_pair[:, 1], shift_pair[:, 1])
    return middle + mixture(second, route_ids, router, weight_in, weight_down)

def reference(tokens, routes, w_qkv, w_out, w_router, ln_gain, ln_shift, expert_in, expert_out, cotangent):

    def forward(stream, proj_qkv, proj_out, router, gains, shifts, weight_in, weight_down):
        for depth in range(LAYERS):
            stream = block(stream, routes[depth], proj_qkv[depth], proj_out[depth], router[depth], gains[depth], shifts[depth], weight_in[depth], weight_down[depth])
        return stream
    output, pullback = jax.vjp(forward, tokens.astype(jnp.float32), w_qkv.astype(jnp.float32), w_out.astype(jnp.float32), w_router.astype(jnp.float32), ln_gain.astype(jnp.float32), ln_shift.astype(jnp.float32), expert_in.astype(jnp.float32), expert_out.astype(jnp.float32))
    gradients = pullback(cotangent.astype(jnp.float32))
    return (output.astype(jnp.bfloat16), gradients[0], gradients[1], gradients[2], gradients[3], gradients[4], gradients[5][:, :, 0], gradients[5][:, :, 1], gradients[6], gradients[7])
```

```python
import functools

import jax
import jax.numpy as jnp
from jax import lax
from jax.experimental import pallas as pl
from jax.experimental.pallas import tpu as pltpu
from jax.sharding import PartitionSpec as P

D = 768
HEAD_DIM = 64
SEQ = 197
LAYERS = 2
LANES = 128
F32 = jnp.float32
BF16 = jnp.bfloat16
NN = (((1,), (0,)), ((), ()))
NT = (((1,), (1,)), ((), ()))
TN = (((0,), (0,)), ((), ()))


def round_up(value, step):
    return -(-value // step) * step


def mm(left, right, dims=NN):
    return lax.dot_general(left, right, dims, preferred_element_type=F32)


def split_low(values):
    high = values.astype(BF16)
    return high, (values - high.astype(F32)).astype(BF16)


def norm_parts(values):
    centred = values - jnp.mean(values, axis=-1, keepdims=True)
    rstd = lax.rsqrt(jnp.mean(centred * centred, axis=-1, keepdims=True) + 1e-06)
    return centred * rstd, rstd


def norm_back(unit, rstd, gain, grad):
    scaled = grad * gain
    return rstd * (
        scaled
        - jnp.mean(scaled, axis=-1, keepdims=True)
        - unit * jnp.mean(scaled * unit, axis=-1, keepdims=True)
    )


def params(mib=48, **more):
    return pltpu.CompilerParams(vmem_limit_bytes=mib * 1024 * 1024, **more)


def head_mask(half):
    lane = lax.broadcasted_iota(jnp.int32, (1, LANES), 1)
    return (lane // HEAD_DIM) == half


def masked(values, keep):
    return jnp.where(keep, values, jnp.zeros_like(values))


def head_probs(query, keys, key_ok):
    scores = mm(query, keys, NT) * (HEAD_DIM**-0.5)
    scores = jnp.where(key_ok, scores, -1e30)
    exponent = jnp.exp(scores - jnp.max(scores, axis=-1, keepdims=True))
    return exponent / jnp.sum(exponent, axis=-1, keepdims=True)


def attn_fwd_kernel(x_ref, w_ref, wo_ref, g_ref, b_ref, normed_ref, packed_ref, heads_ref, part_ref):
    rows = x_ref.shape[0]
    width = wo_ref.shape[1]
    unit, _ = norm_parts(x_ref[...])
    normed = (unit * g_ref[...] + b_ref[...]).astype(BF16)
    normed_ref[...] = normed
    packed_ref[...] = mm(normed, w_ref[...]).astype(BF16)
    key_ok = lax.broadcasted_iota(jnp.int32, (1, rows), 1) < SEQ
    for pair in range(width // LANES):
        low = pair * LANES
        query = packed_ref[:, low : low + LANES]
        keys = packed_ref[:, width + low : width + low + LANES]
        vals = packed_ref[:, 2 * width + low : 2 * width + low + LANES]
        outs = []
        for half in range(2):
            probs = head_probs(masked(query, head_mask(half)), keys, key_ok).astype(BF16)
            outs.append(mm(probs, vals))
        heads_ref[:, low : low + LANES] = jnp.where(head_mask(0), outs[0], outs[1]).astype(BF16)
    part_ref[...] = mm(heads_ref[...], wo_ref[...], NT).astype(BF16)


def weight_specs(width):
    return [
        pl.BlockSpec((D, 3 * width), lambda i: (0, 0)),
        pl.BlockSpec((D, width), lambda i: (0, 3)),
    ]


def rows_spec(rows, cols):
    return pl.BlockSpec((rows, cols), lambda i: (i, 0))


def whole_spec(shape):
    return pl.BlockSpec(shape, lambda i: (0,) * len(shape))


def attn_fwd(stream, gathered, gain, shift, images, width):
    tok = stream.shape[0]
    rows = tok // images
    return pl.pallas_call(
        attn_fwd_kernel,
        grid=(images,),
        in_specs=[rows_spec(rows, D)] + weight_specs(width) + [whole_spec((1, D))] * 2,
        out_specs=[
            rows_spec(rows, D),
            rows_spec(rows, 3 * width),
            rows_spec(rows, width),
            rows_spec(rows, D),
        ],
        out_shape=[
            jax.ShapeDtypeStruct((tok, D), BF16),
            jax.ShapeDtypeStruct((tok, 3 * width), BF16),
            jax.ShapeDtypeStruct((tok, width), BF16),
            jax.ShapeDtypeStruct((tok, D), BF16),
        ],
        compiler_params=params(),
        name="attn_fwd",
    )(stream, gathered, gathered, gain, shift)


def slot_rows(dest_row, start, count, k):
    at = lax.broadcasted_iota(jnp.int32, (count, 1), 0) + start
    return jnp.where(at == dest_row[k : k + 1, :], 1.0, 0.0).astype(BF16)


def slot_cols(dest_col, slots, k):
    at = lax.broadcasted_iota(jnp.int32, (1, slots), 1)
    return jnp.where(at == dest_col[:, k : k + 1], 1.0, 0.0).astype(BF16)


def expert_lane(ids, k):
    lane = lax.broadcasted_iota(jnp.int32, (1, LANES), 1)
    return jnp.where(lane == ids[:, k : k + 1], 1.0, 0.0)


def mid_kernel(
    x_ref, pa_ref, pb_ref, g_ref, b_ref, small_ref, ids_ref, dest_ref,
    middle_ref, act_ref, gates_ref, out_ref,
):
    middle = x_ref[...] + (pa_ref[...].astype(F32) + pb_ref[...].astype(F32))
    middle_ref[...] = middle
    unit, _ = norm_parts(middle)
    act_ref[...] = (unit * g_ref[...] + b_ref[...]).astype(BF16)
    logits = mm(act_ref[...], small_ref[...])
    first = jnp.sum(expert_lane(ids_ref, 0) * logits, axis=-1, keepdims=True)
    second = jnp.sum(expert_lane(ids_ref, 1) * logits, axis=-1, keepdims=True)
    top = jnp.maximum(first, second)
    first, second = jnp.exp(first - top), jnp.exp(second - top)
    total = first + second
    lane = lax.broadcasted_iota(jnp.int32, (1, LANES), 1)
    gates_ref[...] = jnp.where(lane == 0, first / total, jnp.where(lane == 1, second / total, 0.0))
    slots = out_ref.shape[0]
    chunk = slots // 4
    for start in range(0, slots, chunk):
        pick = slot_rows(dest_ref, start, chunk, 0) + slot_rows(dest_ref, start, chunk, 1)
        out_ref[start : start + chunk, :] = mm(pick, act_ref[...]).astype(BF16)


def mid_fwd(stream, own, peer, gain, shift, gathered, ids, dest_row, slots, width):
    tok = stream.shape[0]
    full = whole_spec((tok, D))
    return pl.pallas_call(
        mid_kernel,
        grid=(1,),
        in_specs=[full, full, full, whole_spec((1, D)), whole_spec((1, D))]
        + [pl.BlockSpec((D, LANES), lambda i: (0, 4 * width // LANES))]
        + [whole_spec((tok, 2)), whole_spec((2, tok))],
        out_specs=[full, full, whole_spec((tok, LANES)), whole_spec((slots, D))],
        out_shape=[
            jax.ShapeDtypeStruct((tok, D), F32),
            jax.ShapeDtypeStruct((tok, D), BF16),
            jax.ShapeDtypeStruct((tok, LANES), F32),
            jax.ShapeDtypeStruct((slots, D), BF16),
        ],
        compiler_params=params(),
        name="mid_fwd",
    )(stream, own, peer, gain, shift, gathered, ids, dest_row)


def ffn_fwd_kernel(x_ref, wi_ref, wo_ref, y_ref, act_ref, slope_ref, acc_ref):
    rows, chunk = acc_ref.shape[0], wi_ref.shape[2]
    x = x_ref[...].reshape(rows, D)
    pre = mm(x, wi_ref[0])
    cdf = 0.5 * (1.0 + lax.erf(pre * (0.5**0.5)))
    act = (pre * cdf).astype(BF16)
    slope = cdf + pre * (jnp.exp(-0.5 * pre * pre) * 0.3989422804014327)
    act_ref[...] = act.reshape(act_ref.shape)
    slope_ref[...] = slope.astype(BF16).reshape(slope_ref.shape)
    part = mm(act, wo_ref[0], NT)
    step = pl.program_id(1)

    @pl.when(step == 0)
    def _():
        acc_ref[...] = part

    @pl.when(step > 0)
    def _():
        acc_ref[...] += part

    @pl.when(step == pl.num_programs(1) - 1)
    def _():
        y_ref[...] = acc_ref[...].astype(BF16).reshape(y_ref.shape)


def ffn_specs(shards, cap, chunk):
    token = pl.BlockSpec((shards, 1, cap, D), lambda e, f: (0, e, 0, 0))
    weight = pl.BlockSpec((1, D, chunk), lambda e, f: (e, 0, f))
    hidden = pl.BlockSpec((shards, 1, cap, chunk), lambda e, f: (0, e, 0, f))
    return token, weight, hidden


def ffn_fwd(received, weight_in, weight_down):
    shards, exp_dev, cap, _ = received.shape
    hidden_dev = weight_in.shape[2]
    chunk = 512
    token, weight, hidden = ffn_specs(shards, cap, chunk)
    hidden_shape = jax.ShapeDtypeStruct((shards, exp_dev, cap, hidden_dev), BF16)
    return pl.pallas_call(
        ffn_fwd_kernel,
        grid=(exp_dev, hidden_dev // chunk),
        in_specs=[token, weight, weight],
        out_specs=[token, hidden, hidden],
        out_shape=[jax.ShapeDtypeStruct(received.shape, BF16), hidden_shape, hidden_shape],
        scratch_shapes=[pltpu.VMEM((shards * cap, D), F32)],
        compiler_params=params(),
        name="ffn_fwd",
    )(received, weight_in, weight_down)


def ffn_bwd_kernel(
    xa_ref, xb_ref, da_ref, db_ref, acta_ref, actb_ref, slopea_ref, slopeb_ref, wi_ref, wo_ref,
    dxa_ref, dxb_ref, gi_ref, go_ref, acc_ref,
):
    rows = acc_ref.shape[0]
    half = rows // 2
    chunk = wi_ref.shape[2]

    def both(first, second, cols):
        return jnp.concatenate(
            [first[...].reshape(half, cols), second[...].reshape(half, cols)], axis=0
        )

    x = both(xa_ref, xb_ref, D)
    dy = both(da_ref, db_ref, D)
    act = both(acta_ref, actb_ref, chunk)
    slope = both(slopea_ref, slopeb_ref, chunk)
    dpre = (mm(dy, wo_ref[0]) * slope.astype(F32)).astype(BF16)
    go_ref[0] = mm(dy, act, TN).astype(BF16)
    gi_ref[0] = mm(x, dpre, TN).astype(BF16)
    part = mm(dpre, wi_ref[0], NT)
    step = pl.program_id(1)

    @pl.when(step == 0)
    def _():
        acc_ref[...] = part

    @pl.when(step > 0)
    def _():
        acc_ref[...] += part

    @pl.when(step == pl.num_programs(1) - 1)
    def _():
        dxa_ref[...] = acc_ref[:half].astype(BF16).reshape(dxa_ref.shape)
        dxb_ref[...] = acc_ref[half:].astype(BF16).reshape(dxb_ref.shape)


def ffn_bwd(received, grad_in, act, slope, weight_in, weight_down):
    shards, exp_dev, cap, _ = received[0].shape
    hidden_dev = weight_in.shape[2]
    chunk = 512
    token, weight, hidden = ffn_specs(shards, cap, chunk)
    grad_shape = jax.ShapeDtypeStruct(weight_in.shape, BF16)
    row_shape = jax.ShapeDtypeStruct(received[0].shape, BF16)
    return pl.pallas_call(
        ffn_bwd_kernel,
        grid=(exp_dev, hidden_dev // chunk),
        in_specs=[token] * 4 + [hidden] * 4 + [weight, weight],
        out_specs=[token, token, weight, weight],
        out_shape=[row_shape, row_shape, grad_shape, grad_shape],
        scratch_shapes=[pltpu.VMEM((2 * shards * cap, D), F32)],
        compiler_params=params(),
        name="ffn_bwd",
    )(*received, *grad_in, *act, *slope, weight_in, weight_down)


def combine_kernel(y_ref, dest_ref, gates_ref, taken_ref, part_ref):
    slots = y_ref.shape[0]
    total = None
    for k in range(2):
        picked = mm(slot_cols(dest_ref, slots, k), y_ref[...])
        taken_ref[k] = picked.astype(BF16)
        term = gates_ref[:, k : k + 1] * picked
        total = term if total is None else total + term
    part_ref[...] = total.astype(BF16)


def combine_fwd(returned, dest_col, gates, images):
    slots = returned.shape[0]
    tok = dest_col.shape[0]
    rows = tok // images
    return pl.pallas_call(
        combine_kernel,
        grid=(images,),
        in_specs=[whole_spec((slots, D)), rows_spec(rows, 2), rows_spec(rows, LANES)],
        out_specs=[pl.BlockSpec((2, rows, D), lambda i: (0, i, 0)), rows_spec(rows, D)],
        out_shape=[
            jax.ShapeDtypeStruct((2, tok, D), BF16),
            jax.ShapeDtypeStruct((tok, D), BF16),
        ],
        compiler_params=params(),
        name="combine_fwd",
    )(returned, dest_col, gates)


def spread_kernel(grad_ref, gates_ref, taken_ref, dest_ref, out_ref, pgate_ref):
    grad = grad_ref[...]
    lane = lax.broadcasted_iota(jnp.int32, (1, LANES), 1)
    dys, dots = [], []
    for k in range(2):
        dys.append((gates_ref[:, k : k + 1] * grad).astype(BF16))
        dots.append(jnp.sum(grad * taken_ref[k].astype(F32), axis=-1, keepdims=True))
    pgate_ref[...] = jnp.where(lane == 0, dots[0], jnp.where(lane == 1, dots[1], 0.0)).astype(BF16)
    slots = out_ref.shape[0]
    chunk = slots // 4
    for start in range(0, slots, chunk):
        total = mm(slot_rows(dest_ref, start, chunk, 0), dys[0])
        total = total + mm(slot_rows(dest_ref, start, chunk, 1), dys[1])
        out_ref[start : start + chunk, :] = total.astype(BF16)


def spread_bwd(grad, gates, taken, dest_row, slots):
    tok = grad.shape[0]
    return pl.pallas_call(
        spread_kernel,
        grid=(1,),
        in_specs=[
            whole_spec((tok, D)),
            whole_spec((tok, LANES)),
            whole_spec((2, tok, D)),
            whole_spec((2, tok)),
        ],
        out_specs=[whole_spec((slots, D)), whole_spec((tok, LANES))],
        out_shape=[
            jax.ShapeDtypeStruct((slots, D), BF16),
            jax.ShapeDtypeStruct((tok, LANES), BF16),
        ],
        compiler_params=params(),
        name="spread_bwd",
    )(grad, gates, taken, dest_row)


def gather_kernel(rows_ref, dest_ref, pgate_ref, out_ref):
    slots = rows_ref.shape[0]
    pick = slot_cols(dest_ref, slots, 0) + slot_cols(dest_ref, slots, 1)
    out_ref[:, :D] = mm(pick, rows_ref[...]).astype(BF16)
    out_ref[:, D:] = pgate_ref[...]


def gather_bwd(rows_back, dest_col, pgate, images):
    slots = rows_back.shape[0]
    tok = dest_col.shape[0]
    rows = tok // images
    return pl.pallas_call(
        gather_kernel,
        grid=(images,),
        in_specs=[whole_spec((slots, D)), rows_spec(rows, 2), rows_spec(rows, LANES)],
        out_specs=rows_spec(rows, D + LANES),
        out_shape=jax.ShapeDtypeStruct((tok, D + LANES), BF16),
        compiler_params=params(),
        name="gather_bwd",
    )(rows_back, dest_col, pgate)


def attn_bwd_kernel(
    own_ref, peer_ref, middle_ref, act_ref, gates_ref, ids_ref, grad_ref, normed_ref, packed_ref,
    heads_ref, w_ref, wo_ref, small_ref, g_ref,
    mgrad_ref, pnorm_ref, qkvg_ref, outg_ref, routerg_ref, lng_ref, dpacked_ref,
):
    rows = middle_ref.shape[0]
    width = wo_ref.shape[1]

    @pl.when(pl.program_id(0) == 0)
    def _():
        qkvg_ref[...] = jnp.zeros_like(qkvg_ref)
        outg_ref[...] = jnp.zeros_like(outg_ref)
        routerg_ref[...] = jnp.zeros_like(routerg_ref)
        lng_ref[...] = jnp.zeros_like(lng_ref)

    both = own_ref[...].astype(F32) + peer_ref[...].astype(F32)
    act_grad, dgate = both[:, :D], both[:, D:]
    gates = gates_ref[...]
    chosen = gates * (dgate - jnp.sum(gates * dgate, axis=-1, keepdims=True))
    dlogit = expert_lane(ids_ref, 0) * chosen[:, 0:1] + expert_lane(ids_ref, 1) * chosen[:, 1:2]
    high, low = split_low(dlogit)
    act = act_ref[...]
    routerg_ref[...] += mm(act, high, TN) + mm(act, low, TN)
    act_grad = act_grad + mm(high, small_ref[...], NT) + mm(low, small_ref[...], NT)
    unit, rstd = norm_parts(middle_ref[...])
    lng_ref[0:1, :] += jnp.sum(act_grad * unit, axis=0, keepdims=True)
    lng_ref[1:2, :] += jnp.sum(act_grad, axis=0, keepdims=True)
    mgrad = grad_ref[...] + norm_back(unit, rstd, g_ref[...], act_grad)
    mgrad_ref[...] = mgrad
    attn_grad = mgrad.astype(BF16)
    outg_ref[...] += mm(attn_grad, heads_ref[...], TN)
    dheads = mm(attn_grad, wo_ref[...]).astype(BF16)
    key_ok = lax.broadcasted_iota(jnp.int32, (1, rows), 1) < SEQ
    scale = HEAD_DIM**-0.5
    for pair in range(width // LANES):
        at = pair * LANES
        query = packed_ref[:, at : at + LANES]
        keys = packed_ref[:, width + at : width + at + LANES]
        vals = packed_ref[:, 2 * width + at : 2 * width + at + LANES]
        dhead = dheads[:, at : at + LANES]
        terms = []
        for half in range(2):
            keep = head_mask(half)
            probs = head_probs(masked(query, keep), keys, key_ok)
            dprobs = mm(masked(dhead, keep), vals, NT)
            dscores = probs * (dprobs - jnp.sum(probs * dprobs, axis=-1, keepdims=True))
            dscores = dscores.astype(BF16)
            terms.append(
                (
                    mm(dscores, keys) * scale,
                    mm(dscores, query, TN) * scale,
                    mm(probs.astype(BF16), dhead, TN),
                )
            )
        for part in range(3):
            start = part * width + at
            dpacked_ref[:, start : start + LANES] = jnp.where(
                head_mask(0), terms[0][part], terms[1][part]
            ).astype(BF16)
    qkvg_ref[...] += mm(normed_ref[...], dpacked_ref[...], TN)
    pnorm_ref[...] = mm(dpacked_ref[...], w_ref[...], NT).astype(BF16)


def attn_bwd(own, peer, saved, grad, gathered, gain, ids, images, width):
    middle, act_in, gates, normed, packed, heads = saved
    tok = middle.shape[0]
    rows = tok // images
    return pl.pallas_call(
        attn_bwd_kernel,
        grid=(images,),
        in_specs=[
            rows_spec(rows, D + LANES),
            rows_spec(rows, D + LANES),
            rows_spec(rows, D),
            rows_spec(rows, D),
            rows_spec(rows, LANES),
            rows_spec(rows, 2),
            rows_spec(rows, D),
            rows_spec(rows, D),
            rows_spec(rows, 3 * width),
            rows_spec(rows, width),
        ]
        + weight_specs(width)
        + [pl.BlockSpec((D, LANES), lambda i: (0, 4 * width // LANES)), whole_spec((1, D))],
        out_specs=[
            rows_spec(rows, D),
            rows_spec(rows, D),
            whole_spec((D, 3 * width)),
            whole_spec((D, width)),
            whole_spec((D, LANES)),
            whole_spec((8, D)),
        ],
        out_shape=[
            jax.ShapeDtypeStruct((tok, D), F32),
            jax.ShapeDtypeStruct((tok, D), BF16),
            jax.ShapeDtypeStruct((D, 3 * width), F32),
            jax.ShapeDtypeStruct((D, width), F32),
            jax.ShapeDtypeStruct((D, LANES), F32),
            jax.ShapeDtypeStruct((8, D), F32),
        ],
        scratch_shapes=[pltpu.VMEM((rows, 3 * width), BF16)],
        compiler_params=params(56),
        name="attn_bwd",
    )(
        own, peer, middle, act_in, gates, ids, grad, normed, packed, heads,
        gathered, gathered, gathered, gain,
    )


def swap_cores(values):
    count = lax.axis_size("tensor")
    return lax.ppermute(values, "tensor", [(i, (i + 1) % count) for i in range(count)])


def add_peer(own, far):
    return (own.astype(F32) + swap_cores(far).astype(F32)).astype(BF16)


def over_shard(values, shards, cap):
    return lax.all_to_all(
        values.reshape(shards, -1, cap, D), "shard", split_axis=0, concat_axis=0, tiled=True
    )


def on_device(
    tokens, routes, w_qkv, w_out, w_router, ln_gain, ln_shift, expert_in, expert_out, cotangent
):
    tok_dev = tokens.shape[0]
    images = tok_dev // SEQ
    rows = round_up(SEQ, 16)
    tok = images * rows
    shards = lax.axis_size("shard")
    exp_dev = expert_in.shape[1]
    experts = exp_dev * shards
    cap = round_up(5 * tok_dev // (2 * experts) + 1, 32)
    half_cap = cap // 2
    slots = experts * half_cap
    core = lax.axis_index("tensor")
    width = w_qkv.shape[3]
    block = w_qkv.shape[1]
    all_rows = ("shard", "dp")

    def padded(values, fill=0):
        values = values.reshape((images, SEQ) + values.shape[1:])
        spare = [(0, 0), (0, rows - SEQ)] + [(0, 0)] * (values.ndim - 2)
        return jnp.pad(values, spare, constant_values=fill).reshape((tok,) + values.shape[2:])

    def trimmed(values):
        return values.reshape(images, rows, D)[:, :SEQ].reshape(tok_dev, D)

    gathered, experts_in, experts_out = [], [], []
    for depth in range(LAYERS):
        small = jnp.concatenate([w_router[depth], ln_gain[depth], ln_shift[depth]], axis=1)
        small = jnp.pad(small, ((0, 0), (0, LANES - small.shape[1])))
        pack = jnp.concatenate(
            [w_qkv[depth].reshape(block, 3 * width), w_out[depth], small], axis=1
        )
        gathered.append(lax.all_gather(pack, all_rows, axis=0, tiled=True))
        experts_in.append(lax.all_gather(expert_in[depth], "dp", axis=1, tiled=True))
        experts_out.append(lax.all_gather(expert_out[depth], "dp", axis=1, tiled=True))

    ids, dest_cols, dest_rows = [], [], []
    before = jnp.tril(jnp.ones((tok, tok), BF16), -1)
    for depth in range(LAYERS):
        id_pad = padded(routes[depth], -1)
        hits = id_pad[:, :, None] == jnp.arange(experts, dtype=jnp.int32)[None, None, :]
        count = jnp.sum(hits.astype(F32), axis=1).astype(BF16)
        earlier = jnp.dot(before, count, preferred_element_type=F32)
        slot = jnp.sum(jnp.where(hits, earlier[:, None, :], 0.0), axis=-1).astype(jnp.int32)
        mine = (id_pad >= 0) & (slot % 2 == core)
        dest = jnp.where(mine, id_pad * half_cap + slot // 2, -1)
        ids.append(id_pad)
        dest_cols.append(dest)
        dest_rows.append(dest.T)

    stream = padded(tokens).astype(F32)
    kept = []
    for depth in range(LAYERS):
        pack = gathered[depth]
        vectors = pack[:, 4 * width + experts : 4 * width + experts + 4].astype(F32).T
        gains = (vectors[0:1], vectors[1:2])
        shifts = (vectors[2:3], vectors[3:4])
        normed, packed, heads, part = attn_fwd(stream, pack, gains[0], shifts[0], images, width)
        middle, act_in, gates, outgoing = mid_fwd(
            stream, part, swap_cores(part), gains[1], shifts[1], pack,
            ids[depth], dest_rows[depth], slots, width,
        )
        received = over_shard(outgoing, shards, half_cap)
        received = (received, swap_cores(received))
        own_y, own_act, own_slope = ffn_fwd(received[0], experts_in[depth], experts_out[depth])
        far_y, far_act, far_slope = ffn_fwd(received[1], experts_in[depth], experts_out[depth])
        act, slope = (own_act, far_act), (own_slope, far_slope)
        returned = over_shard(add_peer(own_y, far_y), shards, half_cap).reshape(slots, D)
        taken, mix = combine_fwd(returned, dest_cols[depth], gates, images)
        kept.append(
            (stream, (middle, act_in, gates, normed, packed, heads), received, act, slope, taken, gains)
        )
        stream = middle + (mix.astype(F32) + swap_cores(mix).astype(F32))
    mixed = trimmed(stream.astype(BF16))

    grad = padded(cotangent).astype(F32)
    big, tiny, in_grads, out_grads = [None] * LAYERS, [None] * LAYERS, [None] * LAYERS, [None] * LAYERS
    for depth in reversed(range(LAYERS)):
        stream_in, saved, received, act, slope, taken, gains = kept[depth]
        grad_out, pgate = spread_bwd(grad, saved[2], taken, dest_rows[depth], slots)
        grad_in = over_shard(grad_out, shards, half_cap)
        if depth + 1 < LAYERS:
            grad_in, in_grads[depth + 1], out_grads[depth + 1] = lax.optimization_barrier(
                (grad_in, in_grads[depth + 1], out_grads[depth + 1])
            )
        grad_in = (grad_in, swap_cores(grad_in))
        own_rows, far_rows, in_grad, down_grad = ffn_bwd(
            received, grad_in, act, slope, experts_in[depth], experts_out[depth]
        )
        in_grads[depth] = lax.psum_scatter(in_grad, "dp", scatter_dimension=1, tiled=True)
        out_grads[depth] = lax.psum_scatter(down_grad, "dp", scatter_dimension=1, tiled=True)
        rows_back = over_shard(add_peer(own_rows, far_rows), shards, half_cap).reshape(slots, D)
        part = gather_bwd(rows_back, dest_cols[depth], pgate, images)
        if depth + 1 < LAYERS:
            part, big[depth + 1], in_grads[depth] = lax.optimization_barrier(
                (part, big[depth + 1], in_grads[depth])
            )
        middle_grad, pnorm, qkv_grad, proj_grad, router_grad, second = attn_bwd(
            part, swap_cores(part), saved, grad, gathered[depth], gains[1], ids[depth], images, width
        )
        normed_grad = pnorm.astype(F32) + swap_cores(pnorm).astype(F32)
        unit, rstd = norm_parts(stream_in)
        grad = middle_grad + norm_back(unit, rstd, gains[0], normed_grad)
        vectors = jnp.stack(
            [jnp.sum(normed_grad * unit, axis=0), second[0], jnp.sum(normed_grad, axis=0), second[1]],
            axis=1,
        )
        tiny[depth] = jnp.concatenate([router_grad[:, :experts], vectors], axis=1)
        big[depth] = lax.psum_scatter(
            jnp.concatenate([qkv_grad.astype(BF16), proj_grad.astype(BF16)], axis=1),
            all_rows, scatter_dimension=0, tiled=True,
        ).astype(F32)
    tiny_all = lax.psum_scatter(
        jnp.concatenate(tiny, axis=1), all_rows, scatter_dimension=0, tiled=True
    ).reshape(block, LAYERS, experts + 4)
    tiny_all = jnp.swapaxes(tiny_all, 0, 1)
    big_all = jnp.stack(big, axis=0)
    return (
        mixed,
        trimmed(grad),
        big_all[:, :, : 3 * width].reshape(LAYERS, block, 3, width),
        big_all[:, :, 3 * width :],
        tiny_all[:, :, :experts],
        tiny_all[:, :, experts : experts + 2],
        tiny_all[:, :, experts + 2],
        tiny_all[:, :, experts + 3],
        jnp.stack(in_grads, axis=0).astype(F32),
        jnp.stack(out_grads, axis=0).astype(F32),
    )


def solution(mesh):
    row_split = P(("shard", "dp"), None)
    mid_split = P(None, ("shard", "dp"), None)
    expert_split = P(None, "shard", "dp", "tensor")
    placed = (
        row_split,
        mid_split,
        P(None, ("shard", "dp"), None, "tensor"),
        P(None, ("shard", "dp"), "tensor"),
        mid_split,
        mid_split,
        mid_split,
        expert_split,
        expert_split,
        row_split,
    )
    return jax.shard_map(
        on_device,
        mesh=mesh,
        in_specs=placed,
        out_specs=(
            row_split,
            row_split,
            P(None, ("shard", "dp"), None, "tensor"),
            P(None, ("shard", "dp"), "tensor"),
            mid_split,
            mid_split,
            P(None, ("shard", "dp")),
            P(None, ("shard", "dp")),
            expert_split,
            expert_split,
        ),
        check_vma=False,
    )
```
